32 devices in a mesh: groups: 2 (over y), dp: 4 (over z), tensor: 2 (over x), pipe: 2 (over core).
Axes of the slice: x: 2, y: 2, z: 4, core: 2. Of those that a mesh axis runs over, the one named last changes fastest.
Arguments:
- activations: bfloat16 [8192, 4096], P(('groups', 'dp'), 'tensor'), parts along dimension 0, may hold values from -150 to 150, as said below
- out_grads: bfloat16 [2, 8192, 14336], P('pipe', ('groups', 'dp'), 'tensor'), parts along dimension 1, may hold values from -150 to 150, as said below
- proj_in: bfloat16 [2, 64, 4096], P('pipe', None, 'tensor'), may hold values from -0.09375 to 0.09375
- proj_out: bfloat16 [2, 64, 14336], P('pipe', None, 'tensor'), may hold values from -0.046875 to 0.046875
- sample_ids: int32 [8, 1024], P(('groups', 'dp')), parts along dimension 0, may hold values from 0 to 7, never falling along the last dimension, each value on 1 to 256 neighbouring positions
- queries: bfloat16 [2, 1024, 4096], P('pipe', ('dp', 'tensor')), may hold values from -6 to 6
Outputs:
- scores: float32 [64, 1024], P(('groups', 'dp', 'tensor'), 'pipe'), parts along dimension 0
The draws below stay inside these ranges and needn't reach their ends.
There are 2 independent parts, one for each index of `groups`. The reference program is written for one: setup_inputs(seed, part) draws one part's arguments, and reference() takes and returns one part's arrays. A program takes and returns all parts, laid end to end along the dimension named above; an argument that names none is the same for every part. Nothing has to cross between parts.
Inputs may be any that keep to these rules, and one draw needn't show every extreme that they name: `sample_ids`: each row lists the sample of every token; samples are runs that never fall, every number 0 to 7 appears, each run has 1 to 256 tokens and some run has 256. `activations`: Real-valued. `out_grads`: Real-valued.
All inputs are finite; a program needn't handle non-finite values.
Results may differ from the reference program's by a relative error of at most 0.0078.
Values may be sent and summed in bfloat16 or wider, within the bound.
A program may use at most 128 MiB of HBM per device.

```python
import math
import jax
import jax.numpy as jnp
import numpy as np
from jax import lax

D = 4096
FF = 14336
RANK = 64
PROJ = 2
QN = 1024
TOK_DEV = 1024
SAMP_DEV = 8
FEAT = 4096
BLOCKS = 4
TOKENS = 4096
SAMPLES = 32


def scale_grid(key, lead_count, row_count, col_count):
    key_rows, key_cols = jax.random.split(key)
    row_log = jax.random.uniform(key_rows, (lead_count, row_count, 1), minval=0.0, maxval=math.log(10.0))
    col_log = jax.random.uniform(key_cols, (lead_count, 1, col_count), minval=0.0, maxval=math.log(10.0))
    trend = jnp.arange(row_count, dtype=jnp.float32)[None, :, None] / row_count * math.log(3.0)
    return jnp.exp(row_log + col_log + trend) / 10.0


def draw_activations(key, part):
    key = jax.random.fold_in(key, 11)
    key_scale, key_base = jax.random.split(key, 2)
    scales = scale_grid(key_scale, 1, TOKENS, D)
    base = jnp.clip(jax.random.normal(key_base, (1, TOKENS, D)), -5.0, 5.0)
    return jnp.clip(base * scales, -150.0, 150.0)[0].astype(jnp.bfloat16)


def draw_out_grads(key, part):
    key = jax.random.fold_in(key, 23)
    key_scale, key_base = jax.random.split(key, 2)
    scales = scale_grid(key_scale, PROJ, TOKENS, FF)
    base = jnp.clip(jax.random.normal(key_base, (PROJ, TOKENS, FF)), -5.0, 5.0)
    return jnp.clip(base * scales, -150.0, 150.0).astype(jnp.bfloat16)


def block_levels(key, extent, pieces, least, top_value):
    factor_of, own = 1.0, jax.random.fold_in(key, 6)
    for position, parts in pieces:
        draws = jnp.exp(jax.random.uniform(jax.random.fold_in(own, position), (parts,), jnp.float32, least / len(pieces), top_value / len(pieces)))
        factor_of = factor_of * jnp.repeat(draws, extent[position] // parts).reshape([-1 if axis == position else 1 for axis in range(len(extent))])
    return factor_of


def profile(amount, total, bound, lean):
    loads = [(1 << 20) // math.isqrt(standing ** lean) + 1 for standing in range(2, amount + 1)]
    surplus, holding = total - bound - (amount - 1), [1] * (amount - 1)
    while surplus > 0:
        movable = [i for i in range(amount - 1) if holding[i] < bound]
        mass, remaining = sum([loads[i] for i in movable]), surplus
        for i in movable:
            addition = min(bound - holding[i], max(1, remaining * loads[i] // mass), surplus)
            holding[i] = holding[i] + addition
            surplus = surplus - addition
    return np.array([bound] + holding)


def ragged(rng, number_of, total, reach, lean):
    if number_of == 2:
        one = jax.random.randint(rng, (), max(1, total - reach), min(reach, total - 1) + 1)
        return jnp.stack([one, total - one])
    tallies = jnp.asarray(profile(number_of, total, reach, lean), jnp.int32)
    twos = (number_of - 1) // 2
    giver, receiver = tallies[1:1 + 2 * twos:2], tallies[2:2 + 2 * twos:2]
    slack = jnp.minimum(giver - 1, reach - receiver)
    moved = jax.random.randint(jax.random.fold_in(rng, 1), (twos,), 0, 1 << 20) % (slack + 1)
    tallies = tallies.at[1:1 + 2 * twos:2].set(giver - moved).at[2:2 + 2 * twos:2].set(receiver + moved)
    return tallies[jax.random.permutation(jax.random.fold_in(rng, 2), number_of)]


def gaussian(rng, extent, scale, limit, cuts=(), held_as=jnp.bfloat16):
    gain = block_levels(rng, extent, cuts, -0.22, 0.18) if cuts else 1.0
    entries = jax.random.normal(rng, extent, jnp.float32) * scale * gain
    return jnp.minimum(jnp.maximum(entries, -limit), limit).astype(held_as)


def setup_inputs(seed: int = 0, part: int = 0) -> dict:
    key_of = jax.random.split(jax.random.key(seed), 7)
    part_splits = jax.random.split(jax.random.fold_in(key_of[6], part), 7)
    return {
        "activations": draw_activations(jax.random.fold_in(jax.random.fold_in(key_of[6], part), 71), part),
        "out_grads": draw_out_grads(jax.random.fold_in(jax.random.fold_in(key_of[6], part), 71), part),
        "proj_in": gaussian(key_of[2], (PROJ, RANK, D), D ** -0.5, 0.09375, ((0, 2), (2, 2))),
        "proj_out": gaussian(key_of[3], (PROJ, RANK, FF), FF ** -0.5, 0.046875, ((0, 2), (2, 2))),
        "sample_ids": jax.vmap(lambda own: jnp.searchsorted(jnp.cumsum(ragged(own, SAMP_DEV, TOK_DEV, TOK_DEV // 4, 0)), jnp.arange(TOK_DEV), side="right"))(jax.random.split(part_splits[4], BLOCKS)).reshape((BLOCKS, TOK_DEV)).astype(jnp.int32),
        "queries": gaussian(key_of[5], (PROJ, QN, FEAT), 1.0, 6.0, ((0, 2), (1, 8))),
    }


def damped_inverse(factor):
    order_size = factor.shape[0]
    identity = jnp.eye(order_size, dtype=jnp.float32)
    damped = factor + 0.1 * jnp.trace(factor) / order_size * identity
    lower_factor = jnp.linalg.cholesky(damped)
    return jax.scipy.linalg.cho_solve((lower_factor, True), identity)

def reference(activations, out_grads, proj_in, proj_out, sample_ids, queries):
    offsets = (jnp.arange(BLOCKS, dtype=jnp.int32) * SAMP_DEV)[:, None]
    global_ids = (sample_ids + offsets).reshape(TOKENS).astype(jnp.int32)
    totals = jnp.zeros((SAMPLES, QN), jnp.float32)
    for projection in range(PROJ):
        u_rows = jnp.dot(out_grads[projection].astype(jnp.float32), proj_out[projection].T.astype(jnp.float32), preferred_element_type=jnp.float32).astype(jnp.bfloat16)
        v_rows = jnp.dot(activations.astype(jnp.float32), proj_in[projection].T.astype(jnp.float32), preferred_element_type=jnp.float32).astype(jnp.bfloat16)
        out_factor = jnp.dot(u_rows.T.astype(jnp.float32), u_rows.astype(jnp.float32), preferred_element_type=jnp.float32) / TOKENS
        in_factor = jnp.dot(v_rows.T.astype(jnp.float32), v_rows.astype(jnp.float32), preferred_element_type=jnp.float32) / TOKENS
        inv_out = damped_inverse(out_factor)
        inv_in = damped_inverse(in_factor)
        u_float = u_rows.astype(jnp.float32)
        v_float = v_rows.astype(jnp.float32)
        outer = u_float[:, :, None] * v_float[:, None, :]
        sample_grads = jax.ops.segment_sum(outer, global_ids, num_segments=SAMPLES)
        precond = jnp.einsum('ac,icb->iab', inv_out, sample_grads, precision=lax.Precision.HIGHEST)
        precond = jnp.einsum('iac,cb->iab', precond, inv_in, precision=lax.Precision.HIGHEST)
        precond = precond.astype(jnp.bfloat16).reshape(SAMPLES, FEAT)
        totals = totals + jnp.dot(precond.astype(jnp.float32), queries[projection].T.astype(jnp.float32), preferred_element_type=jnp.float32)
    return totals
```

```python
import functools

import jax
import jax.numpy as jnp
from jax import lax
from jax.experimental import pallas as pl
from jax.experimental.pallas import tpu as pltpu
from jax.sharding import PartitionSpec as P

MESH = pl.DeviceIdType.MESH
SAMP_DEV = 8
NT_DIMS = (((1,), (1,)), ((), ()))
NN_DIMS = (((1,), (0,)), ((), ()))
DAMP = 0.1
NEWTON_STEPS = 7


def dot_nt(a, b):
    return lax.dot_general(a, b, NT_DIMS, preferred_element_type=jnp.float32)


def dot_full(a, b):
    return lax.dot_general(
        a, b, NN_DIMS, precision=lax.Precision.HIGHEST, preferred_element_type=jnp.float32
    )


def each(count, step):
    if count <= 16:
        for i in range(count):
            step(i)
    else:
        lax.fori_loop(0, count, lambda i, c: (step(i), c)[1], 0)


def block_diag(packed, low):
    zero = jnp.zeros_like(packed)
    return jnp.concatenate([jnp.where(low, packed, zero), jnp.where(low, zero, packed)], axis=0)


def kernel(
    n_dp, n_t, dims,
    act, og, w_in, w_out, ids, qry, out,
    og_v, act_v, wi_v, wo_v, ids_v, q_v,
    rs_send, rs_recv, own, uv, fac, sg, sg_recv, inv, pre, pre32, s_send, s_recv,
    in_sem, par_sem, rs_ss, rs_rs, f_ss, f_rs, g_ss, g_rs, p_ss, p_rs, o_ss, o_rs,
):
    rank, tok, chunk, per, q_dev = dims
    n = n_dp * n_t
    half = n // 2
    part = tok // n_t
    n_chunk = part // chunk
    my_dp, my_t, my_p = lax.axis_index("dp"), lax.axis_index("tensor"), lax.axis_index("pipe")
    me = my_dp * n_t + my_t

    def at(index, pipe):
        return {"dp": lax.div(index, n_t), "tensor": lax.rem(index, n_t), "pipe": pipe}

    order = [(s, c) for s in list(range(1, n_t)) + [0] for c in range(n_chunk)]

    def chunk_copies(k):
        s, c = order[k]
        start = pl.multiple_of(lax.rem(my_t + s, n_t) * part + c * chunk, chunk)
        rows = pl.ds(start, chunk)
        return (
            pltpu.make_async_copy(og.at[0, rows, :], og_v.at[k], in_sem.at[0, k]),
            pltpu.make_async_copy(act.at[rows, :], act_v.at[k], in_sem.at[1, k]),
        )

    load_wo = pltpu.make_async_copy(w_out.at[0], wo_v, par_sem.at[0])
    load_wi = pltpu.make_async_copy(w_in.at[0], wi_v, par_sem.at[1])
    load_ids = pltpu.make_async_copy(ids, ids_v, par_sem.at[2])
    load_q = pltpu.make_async_copy(qry.at[0], q_v, par_sem.at[3])
    load_wi.start()
    load_wo.start()
    for k in range(len(order)):
        for copy in chunk_copies(k)[::-1]:
            copy.start()
    load_ids.start()
    load_q.start()

    barrier = pltpu.get_barrier_semaphore()

    def greet(k):
        other = lax.rem(me * 2 + my_p + 1 + k, 2 * n)
        pl.semaphore_signal(
            barrier, inc=1, device_id=at(lax.div(other, 2), lax.rem(other, 2)), device_id_type=MESH
        )

    each(2 * n - 1, greet)

    def rs_copy(k):
        s, c = order[k]
        return pltpu.make_async_remote_copy(
            src_ref=rs_send.at[k], dst_ref=rs_recv.at[k],
            send_sem=rs_ss.at[k], recv_sem=rs_rs.at[k],
            device_id={"tensor": lax.rem(my_t + s, n_t)}, device_id_type=MESH,
        )

    n_send = (n_t - 1) * n_chunk
    load_wi.wait()
    load_wo.wait()
    for k, (s, c) in enumerate(order):
        load_og, load_act = chunk_copies(k)
        load_act.wait()
        part_v = dot_nt(wi_v[...], act_v[k])
        load_og.wait()
        part_u = dot_nt(wo_v[...], og_v[k])
        if s > 0:
            rs_send[k, :rank, :] = part_u.astype(jnp.bfloat16)
            rs_send[k, rank:, :] = part_v.astype(jnp.bfloat16)
            if k == 0:
                pl.semaphore_wait(barrier, 2 * n - 1)
            rs_copy(k).start()
        else:
            own[c, :rank, :] = part_u
            own[c, rank:, :] = part_v

    for k in range(n_send):
        rs_copy(k).wait_recv()
    for c in range(n_chunk):
        total = own[c]
        for s in range(1, n_t):
            total = total + rs_recv[(s - 1) * n_chunk + c].astype(jnp.float32)
        uv[:, c * chunk:(c + 1) * chunk] = total.astype(jnp.bfloat16)

    lane = lax.broadcasted_iota(jnp.int32, (rank, 2 * rank), 1)
    row = lax.broadcasted_iota(jnp.int32, (rank, 2 * rank), 0)
    low = lane < rank
    diag = lax.rem(lane, rank) == row
    both = uv[...]
    square = dot_nt(both, both)
    fac[0] = jnp.where(low, square[:rank], square[rank:])

    def f_copy(s):
        return pltpu.make_async_remote_copy(
            src_ref=fac.at[0], dst_ref=fac.at[s], send_sem=f_ss.at[s], recv_sem=f_rs.at[s],
            device_id=at(lax.rem(me + s, n), my_p), device_id_type=MESH,
        )

    each(n - 1, lambda k: f_copy(k + 1).start())

    load_ids.wait()
    own_ids = ids_v[:, pl.ds(pl.multiple_of(my_t * part, 128), part)]
    u_rows, v_rows = uv[:rank, :], uv[rank:, :]

    def g_copy(s):
        return pltpu.make_async_remote_copy(
            src_ref=sg.at[s], dst_ref=sg_recv.at[s - 1], send_sem=g_ss.at[s - 1], recv_sem=g_rs.at[s - 1],
            device_id={"tensor": lax.rem(my_t + s, n_t)}, device_id_type=MESH,
        )

    wide = max(2, per)
    for s in list(range(1, n_t)) + [0]:
        first = lax.rem(my_t + s, n_t) * per
        masked = jnp.concatenate(
            [jnp.where(own_ids == first + i, v_rows.astype(jnp.float32), 0.0) for i in range(wide)], axis=0
        ).astype(jnp.bfloat16)
        sg[s] = dot_nt(u_rows, masked)
        if s > 0:
            g_copy(s).start()

    each(n - 1, lambda k: f_copy(k + 1).wait_recv())
    if n <= 16:
        factor = fac[0]
        for k in range(1, n):
            factor = factor + fac[k]
    else:
        factor = lax.fori_loop(1, n, lambda k, f: f + fac[k], fac[0])
    factor = factor * (1.0 / (tok * n_dp))
    on_diag = jnp.sum(jnp.where(diag, factor, 0.0), axis=0, keepdims=True)
    lane1 = lax.broadcasted_iota(jnp.int32, (1, 2 * rank), 1)
    trace_a = jnp.sum(jnp.where(lane1 < rank, on_diag, 0.0), axis=1, keepdims=True)
    trace_b = jnp.sum(jnp.where(lane1 < rank, 0.0, on_diag), axis=1, keepdims=True)
    trace = jnp.where(lane1 < rank, trace_a, trace_b)
    eye = jnp.where(diag, 1.0, 0.0)
    damped = factor + (DAMP / rank) * trace * eye
    least = (DAMP / rank) / (1.0 + DAMP / rank)
    alpha = 2.0 / (1.0 + least)
    bound = least * alpha
    scale = alpha / ((1.0 + DAMP / rank) * trace)
    state = jnp.concatenate([damped * scale, eye * scale], axis=0)
    for _ in range(NEWTON_STEPS):
        beta = 2.0 / (1.0 + bound * (2.0 - bound))
        bound = beta * bound * (2.0 - bound)
        state = beta * dot_full(state, block_diag(2.0 * eye - state[:rank], low))
    x = state[rank:]
    t = dot_full(damped, block_diag(x, low))
    x = dot_full(x, block_diag(2.0 * eye - t, low))
    inv[...] = x

    for s in range(1, n_t):
        g_copy(s).wait_recv()
    grads = sg[0]
    for s in range(1, n_t):
        grads = grads + sg_recv[s - 1]
    even = inv[pl.ds(0, rank // 2, stride=2), :]
    odd = inv[pl.ds(1, rank // 2, stride=2), :]
    low_half = low[: rank // 2]
    left = jnp.where(low_half, even, pltpu.roll(odd, rank, 1))
    x_in = jnp.where(low, pltpu.roll(x, rank, 1), x)
    right = block_diag(x_in, low)
    blocks = []
    for m in range(wide // 2):
        pair = grads[:, m * 2 * rank:(m + 1) * 2 * rank]
        swapped = pltpu.roll(pair, rank, 1)
        blocks.append(block_diag(jnp.where(low, pair, swapped), low))
        blocks.append(block_diag(jnp.where(low, swapped, pair), low))
    blocks = blocks[:per]
    mid = dot_full(left, jnp.concatenate(blocks, axis=1))
    mid = jnp.concatenate([mid[:, i * 2 * rank:(i + 1) * 2 * rank] for i in range(per)], axis=0)
    pre[me] = dot_full(mid, right).astype(jnp.bfloat16)

    def p_copy(s):
        return pltpu.make_async_remote_copy(
            src_ref=pre.at[me], dst_ref=pre.at[me], send_sem=p_ss.at[s], recv_sem=p_rs.at[s],
            device_id=at(lax.rem(me + s, n), my_p), device_id_type=MESH,
        )

    each(n - 1, lambda k: p_copy(k + 1).start())
    each(n - 1, lambda k: p_copy(k + 1).wait_recv())

    fine = rank // 2
    total_samples = n * per
    pre32[...] = pre[...].astype(jnp.float32).reshape(total_samples * fine, 2 * rank)
    flat = jnp.concatenate(
        [pre32[pl.ds(a, total_samples, stride=fine), :].astype(jnp.bfloat16) for a in range(fine)], axis=1
    )
    load_q.wait()
    scores = dot_nt(flat, q_v[...])
    for j in range(n):
        s_send[j, :per, :q_dev] = scores[j * per:(j + 1) * per]

    my_half = lax.div(me, half)
    slot = my_p * half + lax.rem(me, half)

    def o_copy(s):
        j = lax.rem(me + s, n)
        return pltpu.make_async_remote_copy(
            src_ref=s_send.at[j], dst_ref=s_recv.at[slot], send_sem=o_ss.at[s], recv_sem=o_rs.at[slot],
            device_id=at(j, my_half), device_id_type=MESH,
        )

    each(n - 1, lambda k: o_copy(k + 1).start())

    @pl.when(my_half == my_p)
    def _():
        s_recv[slot] = s_send[me]

    @pl.when(my_half != my_p)
    def _():
        o_copy(0).start()

    def o_wait(k):
        source = my_p * half + lax.rem(k, half)

        @pl.when(jnp.logical_or(source != me, lax.div(k, half) != my_p))
        def _():
            pltpu.make_async_remote_copy(
                src_ref=s_send.at[0], dst_ref=s_recv.at[k], send_sem=o_ss.at[0], recv_sem=o_rs.at[k],
                device_id=at(lax.rem(me + 1, n), my_p), device_id_type=MESH,
            ).wait_recv()

    each(n, o_wait)
    if q_dev % 128 == 0:
        for k in range(half):
            out[:, k * q_dev:(k + 1) * q_dev] = (s_recv[k] + s_recv[half + k])[:per, :q_dev]
    else:
        out[...] = s_recv[:half] + s_recv[half:]

    for k in range(n_send):
        rs_copy(k).wait_send()
    each(n - 1, lambda k: f_copy(k + 1).wait_send())
    for s in range(1, n_t):
        g_copy(s).wait_send()
    each(n - 1, lambda k: p_copy(k + 1).wait_send())
    each(n - 1, lambda k: o_copy(k + 1).wait_send())

    @pl.when(my_half != my_p)
    def _():
        o_copy(0).wait_send()


def body(n_dp, n_t, activations, out_grads, proj_in, proj_out, sample_ids, queries):
    rank = proj_in.shape[1]
    tok, width = activations.shape
    hidden = out_grads.shape[2]
    q_dev, feat = queries.shape[1:]
    n = n_dp * n_t
    half = n // 2
    per = SAMP_DEV // n_t
    part = tok // n_t
    chunk = min(part, 256)
    n_chunk = part // chunk
    n_all, n_send = n_t * n_chunk, (n_t - 1) * n_chunk
    wide = max(2, per) * rank
    lanes = max(q_dev, 128)
    direct = q_dev % 128 == 0
    out_shape = (per, half * q_dev) if direct else (half, 8, lanes)
    bf16, f32 = jnp.bfloat16, jnp.float32
    dma = pltpu.SemaphoreType.DMA
    result = pl.pallas_call(
        functools.partial(kernel, n_dp, n_t, (rank, tok, chunk, per, q_dev)),
        out_shape=jax.ShapeDtypeStruct(out_shape, f32),
        in_specs=[pl.BlockSpec(memory_space=pl.ANY)] * 6,
        out_specs=pl.BlockSpec(memory_space=pltpu.VMEM),
        scratch_shapes=[
            pltpu.VMEM((n_all, chunk, hidden), bf16),
            pltpu.VMEM((n_all, chunk, width), bf16),
            pltpu.VMEM((rank, width), bf16),
            pltpu.VMEM((rank, hidden), bf16),
            pltpu.VMEM(sample_ids.shape, jnp.int32),
            pltpu.VMEM((q_dev, feat), bf16),
            pltpu.VMEM((n_send, 2 * rank, chunk), bf16),
            pltpu.VMEM((n_send, 2 * rank, chunk), bf16),
            pltpu.VMEM((n_chunk, 2 * rank, chunk), f32),
            pltpu.VMEM((2 * rank, part), bf16),
            pltpu.VMEM((n, rank, 2 * rank), f32),
            pltpu.VMEM((n_t, rank, wide), f32),
            pltpu.VMEM((n_t - 1, rank, wide), f32),
            pltpu.VMEM((rank, 2 * rank), f32),
            pltpu.VMEM((n, per * rank // 2, 2 * rank), bf16),
            pltpu.VMEM((n * per * rank // 2, 2 * rank), f32),
            pltpu.VMEM((n, 8, lanes), f32),
            pltpu.VMEM((n, 8, lanes), f32),
            dma((2, n_all)), dma((4,)),
            dma((n_send,)), dma((n_send,)),
            dma((n,)), dma((n,)),
            dma((n_t - 1,)), dma((n_t - 1,)),
            dma((n,)), dma((n,)),
            dma((n,)), dma((n,)),
        ],
        compiler_params=pltpu.CompilerParams(
            collective_id=0, has_side_effects=True, vmem_limit_bytes=56 * 1024 * 1024
        ),
    )(activations, out_grads, proj_in, proj_out, sample_ids, queries)
    if direct:
        return result
    return result[:, :per, :q_dev].transpose(1, 0, 2).reshape(per, half * q_dev)


def solution(mesh):
    in_specs = (
        P(("groups", "dp"), "tensor"),
        P("pipe", ("groups", "dp"), "tensor"),
        P("pipe", None, "tensor"),
        P("pipe", None, "tensor"),
        P(("groups", "dp"), None),
        P("pipe", ("dp", "tensor"), None),
    )
    out_specs = P(("groups", "dp", "tensor"), "pipe")
    return jax.shard_map(
        functools.partial(body, mesh.shape["dp"], mesh.shape["tensor"]),
        mesh=mesh, in_specs=in_specs, out_specs=out_specs, check_vma=False,
    )
```

```python
import functools

import jax
import jax.numpy as jnp
from jax import lax
from jax.experimental import pallas as pl
from jax.experimental.pallas import tpu as pltpu
from jax.sharding import PartitionSpec as P

MESH = pl.DeviceIdType.MESH
SAMP_DEV = 8
NT_DIMS = (((1,), (1,)), ((), ()))
NN_DIMS = (((1,), (0,)), ((), ()))
DAMP = 0.1
NEWTON_STEPS = 7
PIECES = 1
CHUNK = 256
AHEAD = 4


def dot_nt(a, b):
    return lax.dot_general(a, b, NT_DIMS, preferred_element_type=jnp.float32)


def project(w, x):
    return dot_nt(x, w)


def finish(part):
    return part.T


def dot_full(a, b):
    return lax.dot_general(
        a, b, NN_DIMS, precision=lax.Precision.HIGHEST, preferred_element_type=jnp.float32
    )


def each(count, step):
    if count <= 16:
        for i in range(count):
            step(i)
    else:
        lax.fori_loop(0, count, lambda i, c: (step(i), c)[1], 0)


def block_diag(packed, low):
    zero = jnp.zeros_like(packed)
    return jnp.concatenate([jnp.where(low, packed, zero), jnp.where(low, zero, packed)], axis=0)


def kernel(
    n_dp, n_t, dims,
    act, og, w_in, w_out, ids, qry, out,
    og_v, act_v, wi_v, wo_v, ids_v, q_v,
    rs_send, rs_recv, own, uv, fac, sg, sg_recv, inv, pre, pre32, s_send, s_recv,
    in_sem, par_sem, rs_ss, rs_rs, f_ss, f_rs, g_ss, g_rs, p_ss, p_rs, o_ss, o_rs,
):
    rank, tok, chunk, per, q_dev = dims
    n = n_dp * n_t
    half = n // 2
    part = tok // n_t
    n_chunk = part // chunk
    my_dp, my_t, my_p = lax.axis_index("dp"), lax.axis_index("tensor"), lax.axis_index("pipe")
    me = my_dp * n_t + my_t

    def at(index, pipe):
        return {"dp": lax.div(index, n_t), "tensor": lax.rem(index, n_t), "pipe": pipe}

    order = [(s, c) for s in list(range(1, n_t)) + [0] for c in range(n_chunk)]

    def chunk_copies(k):
        s, c = order[k]
        start = pl.multiple_of(lax.rem(my_t + s, n_t) * part + c * chunk, chunk)
        rows = pl.ds(start, chunk)
        deep = og_v.shape[2] // PIECES
        cuts = [pl.ds(i * deep, deep) for i in range(PIECES)]
        return [pltpu.make_async_copy(act.at[rows, :], act_v.at[k], in_sem.at[PIECES, k])] + [
            pltpu.make_async_copy(og.at[0, rows, cut], og_v.at[k, :, cut], in_sem.at[i, k])
            for i, cut in enumerate(cuts)
        ]

    load_wo = pltpu.make_async_copy(w_out.at[0], wo_v, par_sem.at[0])
    load_wi = pltpu.make_async_copy(w_in.at[0], wi_v, par_sem.at[1])
    load_ids = pltpu.make_async_copy(ids, ids_v, par_sem.at[2])
    load_q = pltpu.make_async_copy(qry.at[0], q_v, par_sem.at[3])
    load_wi.start()
    copies = [copy for k in range(len(order)) for copy in chunk_copies(k)]
    copies = copies[:1] + [load_wo] + copies[1:] + [load_ids, load_q]
    for copy in copies[:AHEAD]:
        copy.start()
    arrived = [0]

    def take():
        i = arrived[0]
        copies[i].wait()
        if i + AHEAD < len(copies):
            copies[i + AHEAD].start()
        arrived[0] = i + 1

    barrier = pltpu.get_barrier_semaphore()

    def greet(k):
        other = lax.rem(me * 2 + my_p + 1 + k, 2 * n)
        pl.semaphore_signal(
            barrier, inc=1, device_id=at(lax.div(other, 2), lax.rem(other, 2)), device_id_type=MESH
        )

    each(2 * n - 1, greet)

    def rs_copy(k):
        s, c = order[k]
        return pltpu.make_async_remote_copy(
            src_ref=rs_send.at[k], dst_ref=rs_recv.at[k],
            send_sem=rs_ss.at[k], recv_sem=rs_rs.at[k],
            device_id={"tensor": lax.rem(my_t + s, n_t)}, device_id_type=MESH,
        )

    n_send = (n_t - 1) * n_chunk
    ready = min(n_send, 2) - 1
    load_wi.wait()
    for k, (s, c) in enumerate(order):
        take()
        part_v = project(wi_v[...], act_v[k])
        if k == 0:
            take()
        part_u = 0.0
        deep = og_v.shape[2] // PIECES
        for i in range(PIECES):
            take()
            cut = slice(i * deep, (i + 1) * deep)
            part_u = part_u + project(wo_v[:, cut], og_v[k, :, cut])
        part_u, part_v = finish(part_u), finish(part_v)
        if s > 0:
            rs_send[k, :rank, :] = part_u.astype(jnp.bfloat16)
            rs_send[k, rank:, :] = part_v.astype(jnp.bfloat16)
            if k == ready:
                pl.semaphore_wait(barrier, 2 * n - 1)
                for earlier in range(k):
                    rs_copy(earlier).start()
            if k >= ready:
                rs_copy(k).start()
        else:
            own[c, :rank, :] = part_u
            own[c, rank:, :] = part_v

    for k in range(n_send):
        rs_copy(k).wait_recv()
    for c in range(n_chunk):
        total = own[c]
        for s in range(1, n_t):
            total = total + rs_recv[(s - 1) * n_chunk + c].astype(jnp.float32)
        uv[:, c * chunk:(c + 1) * chunk] = total.astype(jnp.bfloat16)

    lane = lax.broadcasted_iota(jnp.int32, (rank, 2 * rank), 1)
    row = lax.broadcasted_iota(jnp.int32, (rank, 2 * rank), 0)
    low = lane < rank
    diag = lax.rem(lane, rank) == row
    both = uv[...]
    square = dot_nt(both, both)
    fac[0] = jnp.where(low, square[:rank], square[rank:])

    def f_copy(s):
        return pltpu.make_async_remote_copy(
            src_ref=fac.at[0], dst_ref=fac.at[s], send_sem=f_ss.at[s], recv_sem=f_rs.at[s],
            device_id=at(lax.rem(me + s, n), my_p), device_id_type=MESH,
        )

    each(n - 1, lambda k: f_copy(k + 1).start())

    take()
    own_ids = ids_v[:, pl.ds(pl.multiple_of(my_t * part, 128), part)]
    u_rows, v_rows = uv[:rank, :], uv[rank:, :]

    def g_copy(s):
        return pltpu.make_async_remote_copy(
            src_ref=sg.at[s], dst_ref=sg_recv.at[s - 1], send_sem=g_ss.at[s - 1], recv_sem=g_rs.at[s - 1],
            device_id={"tensor": lax.rem(my_t + s, n_t)}, device_id_type=MESH,
        )

    wide = max(2, per)
    for s in list(range(1, n_t)) + [0]:
        first = lax.rem(my_t + s, n_t) * per
        masked = jnp.concatenate(
            [jnp.where(own_ids == first + i, v_rows.astype(jnp.float32), 0.0) for i in range(wide)], axis=0
        ).astype(jnp.bfloat16)
        sg[s] = dot_nt(u_rows, masked)
        if s > 0:
            g_copy(s).start()

    each(n - 1, lambda k: f_copy(k + 1).wait_recv())
    if n <= 16:
        factor = fac[0]
        for k in range(1, n):
            factor = factor + fac[k]
    else:
        factor = lax.fori_loop(1, n, lambda k, f: f + fac[k], fac[0])
    factor = factor * (1.0 / (tok * n_dp))
    on_diag = jnp.sum(jnp.where(diag, factor, 0.0), axis=0, keepdims=True)
    lane1 = lax.broadcasted_iota(jnp.int32, (1, 2 * rank), 1)
    trace_a = jnp.sum(jnp.where(lane1 < rank, on_diag, 0.0), axis=1, keepdims=True)
    trace_b = jnp.sum(jnp.where(lane1 < rank, 0.0, on_diag), axis=1, keepdims=True)
    trace = jnp.where(lane1 < rank, trace_a, trace_b)
    eye = jnp.where(diag, 1.0, 0.0)
    damped = factor + (DAMP / rank) * trace * eye
    least = (DAMP / rank) / (1.0 + DAMP / rank)
    alpha = 2.0 / (1.0 + least)
    bound = least * alpha
    scale = alpha / ((1.0 + DAMP / rank) * trace)
    state = jnp.concatenate([damped * scale, eye * scale], axis=0)
    for _ in range(NEWTON_STEPS):
        beta = 2.0 / (1.0 + bound * (2.0 - bound))
        bound = beta * bound * (2.0 - bound)
        state = beta * dot_full(state, block_diag(2.0 * eye - state[:rank], low))
    x = state[rank:]
    t = dot_full(damped, block_diag(x, low))
    x = dot_full(x, block_diag(2.0 * eye - t, low))
    inv[...] = x

    for s in range(1, n_t):
        g_copy(s).wait_recv()
    grads = sg[0]
    for s in range(1, n_t):
        grads = grads + sg_recv[s - 1]
    even = inv[pl.ds(0, rank // 2, stride=2), :]
    odd = inv[pl.ds(1, rank // 2, stride=2), :]
    low_half = low[: rank // 2]
    left = jnp.where(low_half, even, pltpu.roll(odd, rank, 1))
    x_in = jnp.where(low, pltpu.roll(x, rank, 1), x)
    right = block_diag(x_in, low)
    blocks = []
    for m in range(wide // 2):
        pair = grads[:, m * 2 * rank:(m + 1) * 2 * rank]
        swapped = pltpu.roll(pair, rank, 1)
        blocks.append(block_diag(jnp.where(low, pair, swapped), low))
        blocks.append(block_diag(jnp.where(low, swapped, pair), low))
    blocks = blocks[:per]
    mid = dot_full(left, jnp.concatenate(blocks, axis=1))
    mid = jnp.concatenate([mid[:, i * 2 * rank:(i + 1) * 2 * rank] for i in range(per)], axis=0)
    pre[me] = dot_full(mid, right).astype(jnp.bfloat16)

    def p_copy(s):
        return pltpu.make_async_remote_copy(
            src_ref=pre.at[me], dst_ref=pre.at[me], send_sem=p_ss.at[s], recv_sem=p_rs.at[s],
            device_id=at(lax.rem(me + s, n), my_p), device_id_type=MESH,
        )

    each(n - 1, lambda k: p_copy(k + 1).start())
    each(n - 1, lambda k: p_copy(k + 1).wait_recv())

    fine = rank // 2
    total_samples = n * per
    pre32[...] = pre[...].astype(jnp.float32).reshape(total_samples * fine, 2 * rank)
    flat = jnp.concatenate(
        [pre32[pl.ds(a, total_samples, stride=fine), :].astype(jnp.bfloat16) for a in range(fine)], axis=1
    )
    take()
    scores = dot_nt(flat, q_v[...])
    for j in range(n):
        s_send[j, :per, :q_dev] = scores[j * per:(j + 1) * per]

    my_half = lax.div(me, half)
    slot = my_p * half + lax.rem(me, half)

    def o_copy(s):
        j = lax.rem(me + s, n)
        return pltpu.make_async_remote_copy(
            src_ref=s_send.at[j], dst_ref=s_recv.at[slot], send_sem=o_ss.at[s], recv_sem=o_rs.at[slot],
            device_id=at(j, my_half), device_id_type=MESH,
        )

    each(n - 1, lambda k: o_copy(k + 1).start())

    @pl.when(my_half == my_p)
    def _():
        s_recv[slot] = s_send[me]

    @pl.when(my_half != my_p)
    def _():
        o_copy(0).start()

    def o_wait(k):
        source = my_p * half + lax.rem(k, half)

        @pl.when(jnp.logical_or(source != me, lax.div(k, half) != my_p))
        def _():
            pltpu.make_async_remote_copy(
                src_ref=s_send.at[0], dst_ref=s_recv.at[k], send_sem=o_ss.at[0], recv_sem=o_rs.at[k],
                device_id=at(lax.rem(me + 1, n), my_p), device_id_type=MESH,
            ).wait_recv()

    each(n, o_wait)
    if q_dev % 128 == 0:
        for k in range(half):
            out[:, k * q_dev:(k + 1) * q_dev] = (s_recv[k] + s_recv[half + k])[:per, :q_dev]
    else:
        out[...] = s_recv[:half] + s_recv[half:]

    for k in range(n_send):
        rs_copy(k).wait_send()
    each(n - 1, lambda k: f_copy(k + 1).wait_send())
    for s in range(1, n_t):
        g_copy(s).wait_send()
    each(n - 1, lambda k: p_copy(k + 1).wait_send())
    each(n - 1, lambda k: o_copy(k + 1).wait_send())

    @pl.when(my_half != my_p)
    def _():
        o_copy(0).wait_send()


def body(n_dp, n_t, activations, out_grads, proj_in, proj_out, sample_ids, queries):
    rank = proj_in.shape[1]
    tok, width = activations.shape
    hidden = out_grads.shape[2]
    q_dev, feat = queries.shape[1:]
    n = n_dp * n_t
    half = n // 2
    per = SAMP_DEV // n_t
    part = tok // n_t
    chunk = min(part, CHUNK)
    n_chunk = part // chunk
    n_all, n_send = n_t * n_chunk, (n_t - 1) * n_chunk
    wide = max(2, per) * rank
    lanes = max(q_dev, 128)
    direct = q_dev % 128 == 0
    out_shape = (per, half * q_dev) if direct else (half, 8, lanes)
    bf16, f32 = jnp.bfloat16, jnp.float32
    dma = pltpu.SemaphoreType.DMA
    result = pl.pallas_call(
        functools.partial(kernel, n_dp, n_t, (rank, tok, chunk, per, q_dev)),
        out_shape=jax.ShapeDtypeStruct(out_shape, f32),
        in_specs=[pl.BlockSpec(memory_space=pl.ANY)] * 6,
        out_specs=pl.BlockSpec(memory_space=pltpu.VMEM),
        scratch_shapes=[
            pltpu.VMEM((n_all, chunk, hidden), bf16),
            pltpu.VMEM((n_all, chunk, width), bf16),
            pltpu.VMEM((rank, width), bf16),
            pltpu.VMEM((rank, hidden), bf16),
            pltpu.VMEM(sample_ids.shape, jnp.int32),
            pltpu.VMEM((q_dev, feat), bf16),
            pltpu.VMEM((n_send, 2 * rank, chunk), bf16),
            pltpu.VMEM((n_send, 2 * rank, chunk), bf16),
            pltpu.VMEM((n_chunk, 2 * rank, chunk), f32),
            pltpu.VMEM((2 * rank, part), bf16),
            pltpu.VMEM((n, rank, 2 * rank), f32),
            pltpu.VMEM((n_t, rank, wide), f32),
            pltpu.VMEM((n_t - 1, rank, wide), f32),
            pltpu.VMEM((rank, 2 * rank), f32),
            pltpu.VMEM((n, per * rank // 2, 2 * rank), bf16),
            pltpu.VMEM((n * per * rank // 2, 2 * rank), f32),
            pltpu.VMEM((n, 8, lanes), f32),
            pltpu.VMEM((n, 8, lanes), f32),
            dma((PIECES + 1, n_all)), dma((4,)),
            dma((n_send,)), dma((n_send,)),
            dma((n,)), dma((n,)),
            dma((n_t - 1,)), dma((n_t - 1,)),
            dma((n,)), dma((n,)),
            dma((n,)), dma((n,)),
        ],
        compiler_params=pltpu.CompilerParams(
            collective_id=0, has_side_effects=True, vmem_limit_bytes=56 * 1024 * 1024
        ),
    )(activations, out_grads, proj_in, proj_out, sample_ids, queries)
    if direct:
        return result
    return result[:, :per, :q_dev].transpose(1, 0, 2).reshape(per, half * q_dev)


def solution(mesh):
    in_specs = (
        P(("groups", "dp"), "tensor"),
        P("pipe", ("groups", "dp"), "tensor"),
        P("pipe", None, "tensor"),
        P("pipe", None, "tensor"),
        P(("groups", "dp"), None),
        P("pipe", ("dp", "tensor"), None),
    )
    out_specs = P(("groups", "dp", "tensor"), "pipe")
    return jax.shard_map(
        functools.partial(body, mesh.shape["dp"], mesh.shape["tensor"]),
        mesh=mesh, in_specs=in_specs, out_specs=out_specs, check_vma=False,
    )
```

```python
import functools

import jax
import jax.numpy as jnp
from jax import lax
from jax.experimental import pallas as pl
from jax.experimental.pallas import tpu as pltpu
from jax.sharding import PartitionSpec as P

MESH = pl.DeviceIdType.MESH
SAMP_DEV = 8
NT_DIMS = (((1,), (1,)), ((), ()))
NN_DIMS = (((1,), (0,)), ((), ()))
DAMP = 0.1
NEWTON_STEPS = 7
PIECES = 1
CHUNK = 256
AHEAD = 4


def dot_nt(a, b):
    return lax.dot_general(a, b, NT_DIMS, preferred_element_type=jnp.float32)


def project(w, x):
    return dot_nt(x, w)


def finish(part):
    return part.T


def dot_full(a, b):
    return lax.dot_general(
        a, b, NN_DIMS, precision=lax.Precision.HIGHEST, preferred_element_type=jnp.float32
    )


def each(count, step):
    if count <= 16:
        for i in range(count):
            step(i)
    else:
        lax.fori_loop(0, count, lambda i, c: (step(i), c)[1], 0)


def block_diag(packed, low):
    zero = jnp.zeros_like(packed)
    return jnp.concatenate([jnp.where(low, packed, zero), jnp.where(low, zero, packed)], axis=0)


def kernel(
    n_dp, n_t, dims,
    act, og, w_in, w_out, ids, qry, out,
    og_v, act_v, wi_v, wo_v, ids_v, q_v,
    rs_send, rs_recv, own, uv, fac, sg, sg_recv, inv, pre, pre32, s_send, s_recv,
    in_sem, par_sem, rs_ss, rs_rs, f_ss, f_rs, g_ss, g_rs, p_ss, p_rs, o_ss, o_rs,
):
    rank, tok, chunk, per, q_dev = dims
    n = n_dp * n_t
    half = n // 2
    part = tok // n_t
    n_chunk = part // chunk
    my_dp, my_t, my_p = lax.axis_index("dp"), lax.axis_index("tensor"), lax.axis_index("pipe")
    me = my_dp * n_t + my_t

    def at(index, pipe):
        return {"dp": lax.div(index, n_t), "tensor": lax.rem(index, n_t), "pipe": pipe}

    order = [(s, c) for s in list(range(1, n_t)) + [0] for c in range(n_chunk)]

    def chunk_copies(k):
        s, c = order[k]
        start = pl.multiple_of(lax.rem(my_t + s, n_t) * part + c * chunk, chunk)
        rows = pl.ds(start, chunk)
        deep = og_v.shape[2] // PIECES
        cuts = [pl.ds(i * deep, deep) for i in range(PIECES)]
        return [pltpu.make_async_copy(act.at[rows, :], act_v.at[k], in_sem.at[PIECES, k])] + [
            pltpu.make_async_copy(og.at[0, rows, cut], og_v.at[k, :, cut], in_sem.at[i, k])
            for i, cut in enumerate(cuts)
        ]

    load_wo = pltpu.make_async_copy(w_out.at[0], wo_v, par_sem.at[0])
    load_wi = pltpu.make_async_copy(w_in.at[0], wi_v, par_sem.at[1])
    load_ids = pltpu.make_async_copy(ids, ids_v, par_sem.at[2])
    load_q = pltpu.make_async_copy(qry.at[0], q_v, par_sem.at[3])
    load_wi.start()
    copies = [copy for k in range(len(order)) for copy in chunk_copies(k)]
    copies = copies[:1] + [load_wo] + copies[1:] + [load_ids, load_q]
    for copy in copies[:AHEAD]:
        copy.start()
    arrived = [0]

    def take():
        i = arrived[0]
        copies[i].wait()
        if i + AHEAD < len(copies):
            copies[i + AHEAD].start()
        arrived[0] = i + 1

    barrier = pltpu.get_barrier_semaphore()

    def greet(k):
        other = lax.rem(me * 2 + my_p + 1 + k, 2 * n)
        pl.semaphore_signal(
            barrier, inc=1, device_id=at(lax.div(other, 2), lax.rem(other, 2)), device_id_type=MESH
        )

    each(2 * n - 1, greet)

    def rs_copy(k):
        s, c = order[k]
        return pltpu.make_async_remote_copy(
            src_ref=rs_send.at[k], dst_ref=rs_recv.at[k],
            send_sem=rs_ss.at[k], recv_sem=rs_rs.at[k],
            device_id={"tensor": lax.rem(my_t + s, n_t)}, device_id_type=MESH,
        )

    n_send = (n_t - 1) * n_chunk
    ready = min(n_send, 2) - 1
    load_wi.wait()
    for k, (s, c) in enumerate(order):
        take()
        part_v = project(wi_v[...], act_v[k])
        if k == 0:
            take()
        part_u = 0.0
        deep = og_v.shape[2] // PIECES
        for i in range(PIECES):
            take()
            cut = slice(i * deep, (i + 1) * deep)
            part_u = part_u + project(wo_v[:, cut], og_v[k, :, cut])
        part_u, part_v = finish(part_u), finish(part_v)
        if s > 0:
            rs_send[k, :rank, :] = part_u.astype(jnp.bfloat16)
            rs_send[k, rank:, :] = part_v.astype(jnp.bfloat16)
            if k == ready:
                pl.semaphore_wait(barrier, 2 * n - 1)
                for earlier in range(k):
                    rs_copy(earlier).start()
            if k >= ready:
                rs_copy(k).start()
        else:
            own[c, :rank, :] = part_u
            own[c, rank:, :] = part_v

    for k in range(n_send):
        rs_copy(k).wait_recv()
    for c in range(n_chunk):
        total = own[c]
        for s in range(1, n_t):
            total = total + rs_recv[(s - 1) * n_chunk + c].astype(jnp.float32)
        uv[:, c * chunk:(c + 1) * chunk] = total.astype(jnp.bfloat16)

    lane = lax.broadcasted_iota(jnp.int32, (rank, 2 * rank), 1)
    row = lax.broadcasted_iota(jnp.int32, (rank, 2 * rank), 0)
    low = lane < rank
    column = lax.rem(lane, rank)
    diag = column == row
    low_half = low[: rank // 2]
    both = uv[...]
    square = dot_nt(both, both)
    packed = jnp.where(low, square[:rank], square[rank:])
    other = pltpu.roll(packed, rank, 1)
    mixed = jnp.where(low == (row < column), packed, other)
    first_diag = jnp.sum(jnp.where(diag, packed, 0.0), axis=0, keepdims=True)
    fac[0, : rank // 2, :] = jnp.where(low_half, mixed[: rank // 2], mixed[rank // 2:])
    fac[0, rank // 2:, :] = jnp.broadcast_to(first_diag, (8, 2 * rank))

    def f_copy(s):
        return pltpu.make_async_remote_copy(
            src_ref=fac.at[0], dst_ref=fac.at[s], send_sem=f_ss.at[s], recv_sem=f_rs.at[s],
            device_id=at(lax.rem(me + s, n), my_p), device_id_type=MESH,
        )

    each(n - 1, lambda k: f_copy(k + 1).start())

    take()
    own_ids = ids_v[:, pl.ds(pl.multiple_of(my_t * part, 128), part)]
    u_rows, v_rows = uv[:rank, :], uv[rank:, :]

    def g_copy(s):
        return pltpu.make_async_remote_copy(
            src_ref=sg.at[s], dst_ref=sg_recv.at[s - 1], send_sem=g_ss.at[s - 1], recv_sem=g_rs.at[s - 1],
            device_id={"tensor": lax.rem(my_t + s, n_t)}, device_id_type=MESH,
        )

    wide = max(2, per)
    for s in list(range(1, n_t)) + [0]:
        first = lax.rem(my_t + s, n_t) * per
        masked = jnp.concatenate(
            [jnp.where(own_ids == first + i, v_rows.astype(jnp.float32), 0.0) for i in range(wide)], axis=0
        ).astype(jnp.bfloat16)
        sg[s] = dot_nt(u_rows, masked)
        if s > 0:
            g_copy(s).start()

    each(n - 1, lambda k: f_copy(k + 1).wait_recv())
    if n <= 16:
        factor = fac[0]
        for k in range(1, n):
            factor = factor + fac[k]
    else:
        factor = lax.fori_loop(1, n, lambda k, f: f + fac[k], fac[0])
    folded = factor[: rank // 2]
    turned = pltpu.roll(folded, rank, 1)
    mixed = jnp.concatenate(
        [jnp.where(low_half, folded, turned), jnp.where(low_half, turned, folded)], axis=0
    )
    mirrored = jnp.concatenate([mixed, mixed], axis=0).T[:rank]
    first_diag = factor[rank // 2: rank // 2 + 1]
    factor = jnp.where(low == (row < column), mixed, mirrored)
    factor = jnp.where(diag, jnp.where(low, first_diag, mixed), factor)
    factor = factor * (1.0 / (tok * n_dp))
    on_diag = jnp.sum(jnp.where(diag, factor, 0.0), axis=0, keepdims=True)
    lane1 = lax.broadcasted_iota(jnp.int32, (1, 2 * rank), 1)
    trace_a = jnp.sum(jnp.where(lane1 < rank, on_diag, 0.0), axis=1, keepdims=True)
    trace_b = jnp.sum(jnp.where(lane1 < rank, 0.0, on_diag), axis=1, keepdims=True)
    trace = jnp.where(lane1 < rank, trace_a, trace_b)
    eye = jnp.where(diag, 1.0, 0.0)
    damped = factor + (DAMP / rank) * trace * eye
    least = (DAMP / rank) / (1.0 + DAMP / rank)
    alpha = 2.0 / (1.0 + least)
    bound = least * alpha
    scale = alpha / ((1.0 + DAMP / rank) * trace)
    state = jnp.concatenate([damped * scale, eye * scale], axis=0)
    for _ in range(NEWTON_STEPS):
        beta = 2.0 / (1.0 + bound * (2.0 - bound))
        bound = beta * bound * (2.0 - bound)
        state = beta * dot_full(state, block_diag(2.0 * eye - state[:rank], low))
    x = state[rank:]
    t = dot_full(damped, block_diag(x, low))
    x = dot_full(x, block_diag(2.0 * eye - t, low))
    inv[...] = x

    for s in range(1, n_t):
        g_copy(s).wait_recv()
    grads = sg[0]
    for s in range(1, n_t):
        grads = grads + sg_recv[s - 1]
    even = inv[pl.ds(0, rank // 2, stride=2), :]
    odd = inv[pl.ds(1, rank // 2, stride=2), :]
    left = jnp.where(low_half, even, pltpu.roll(odd, rank, 1))
    x_in = jnp.where(low, pltpu.roll(x, rank, 1), x)
    right = block_diag(x_in, low)
    blocks = []
    for m in range(wide // 2):
        pair = grads[:, m * 2 * rank:(m + 1) * 2 * rank]
        swapped = pltpu.roll(pair, rank, 1)
        blocks.append(block_diag(jnp.where(low, pair, swapped), low))
        blocks.append(block_diag(jnp.where(low, swapped, pair), low))
    blocks = blocks[:per]
    mid = dot_full(left, jnp.concatenate(blocks, axis=1))
    mid = jnp.concatenate([mid[:, i * 2 * rank:(i + 1) * 2 * rank] for i in range(per)], axis=0)
    pre[me] = dot_full(mid, right).astype(jnp.bfloat16)

    def p_copy(s):
        return pltpu.make_async_remote_copy(
            src_ref=pre.at[me], dst_ref=pre.at[me], send_sem=p_ss.at[s], recv_sem=p_rs.at[s],
            device_id=at(lax.rem(me + s, n), my_p), device_id_type=MESH,
        )

    each(n - 1, lambda k: p_copy(k + 1).start())
    each(n - 1, lambda k: p_copy(k + 1).wait_recv())

    fine = rank // 2
    total_samples = n * per
    pre32[...] = pre[...].astype(jnp.float32).reshape(total_samples * fine, 2 * rank)
    flat = jnp.concatenate(
        [pre32[pl.ds(a, total_samples, stride=fine), :].astype(jnp.bfloat16) for a in range(fine)], axis=1
    )
    take()
    scores = dot_nt(flat, q_v[...])
    for j in range(n):
        s_send[j, :per, :q_dev] = scores[j * per:(j + 1) * per]

    my_half = lax.div(me, half)
    slot = my_p * half + lax.rem(me, half)

    def o_copy(s):
        j = lax.rem(me + s, n)
        return pltpu.make_async_remote_copy(
            src_ref=s_send.at[j], dst_ref=s_recv.at[slot], send_sem=o_ss.at[s], recv_sem=o_rs.at[slot],
            device_id=at(j, my_half), device_id_type=MESH,
        )

    each(n - 1, lambda k: o_copy(k + 1).start())

    @pl.when(my_half == my_p)
    def _():
        s_recv[slot] = s_send[me]

    @pl.when(my_half != my_p)
    def _():
        o_copy(0).start()

    def o_wait(k):
        source = my_p * half + lax.rem(k, half)

        @pl.when(jnp.logical_or(source != me, lax.div(k, half) != my_p))
        def _():
            pltpu.make_async_remote_copy(
                src_ref=s_send.at[0], dst_ref=s_recv.at[k], send_sem=o_ss.at[0], recv_sem=o_rs.at[k],
                device_id=at(lax.rem(me + 1, n), my_p), device_id_type=MESH,
            ).wait_recv()

    each(n, o_wait)
    if q_dev % 128 == 0:
        for k in range(half):
            out[:, k * q_dev:(k + 1) * q_dev] = (s_recv[k] + s_recv[half + k])[:per, :q_dev]
    else:
        out[...] = s_recv[:half] + s_recv[half:]

    for k in range(n_send):
        rs_copy(k).wait_send()
    each(n - 1, lambda k: f_copy(k + 1).wait_send())
    for s in range(1, n_t):
        g_copy(s).wait_send()
    each(n - 1, lambda k: p_copy(k + 1).wait_send())
    each(n - 1, lambda k: o_copy(k + 1).wait_send())

    @pl.when(my_half != my_p)
    def _():
        o_copy(0).wait_send()


def body(n_dp, n_t, activations, out_grads, proj_in, proj_out, sample_ids, queries):
    rank = proj_in.shape[1]
    tok, width = activations.shape
    hidden = out_grads.shape[2]
    q_dev, feat = queries.shape[1:]
    n = n_dp * n_t
    half = n // 2
    per = SAMP_DEV // n_t
    part = tok // n_t
    chunk = min(part, CHUNK)
    n_chunk = part // chunk
    n_all, n_send = n_t * n_chunk, (n_t - 1) * n_chunk
    wide = max(2, per) * rank
    lanes = max(q_dev, 128)
    direct = q_dev % 128 == 0
    out_shape = (per, half * q_dev) if direct else (half, 8, lanes)
    bf16, f32 = jnp.bfloat16, jnp.float32
    dma = pltpu.SemaphoreType.DMA
    result = pl.pallas_call(
        functools.partial(kernel, n_dp, n_t, (rank, tok, chunk, per, q_dev)),
        out_shape=jax.ShapeDtypeStruct(out_shape, f32),
        in_specs=[pl.BlockSpec(memory_space=pl.ANY)] * 6,
        out_specs=pl.BlockSpec(memory_space=pltpu.VMEM),
        scratch_shapes=[
            pltpu.VMEM((n_all, chunk, hidden), bf16),
            pltpu.VMEM((n_all, chunk, width), bf16),
            pltpu.VMEM((rank, width), bf16),
            pltpu.VMEM((rank, hidden), bf16),
            pltpu.VMEM(sample_ids.shape, jnp.int32),
            pltpu.VMEM((q_dev, feat), bf16),
            pltpu.VMEM((n_send, 2 * rank, chunk), bf16),
            pltpu.VMEM((n_send, 2 * rank, chunk), bf16),
            pltpu.VMEM((n_chunk, 2 * rank, chunk), f32),
            pltpu.VMEM((2 * rank, part), bf16),
            pltpu.VMEM((n, rank // 2 + 8, 2 * rank), f32),
            pltpu.VMEM((n_t, rank, wide), f32),
            pltpu.VMEM((n_t - 1, rank, wide), f32),
            pltpu.VMEM((rank, 2 * rank), f32),
            pltpu.VMEM((n, per * rank // 2, 2 * rank), bf16),
            pltpu.VMEM((n * per * rank // 2, 2 * rank), f32),
            pltpu.VMEM((n, 8, lanes), f32),
            pltpu.VMEM((n, 8, lanes), f32),
            dma((PIECES + 1, n_all)), dma((4,)),
            dma((n_send,)), dma((n_send,)),
            dma((n,)), dma((n,)),
            dma((n_t - 1,)), dma((n_t - 1,)),
            dma((n,)), dma((n,)),
            dma((n,)), dma((n,)),
        ],
        compiler_params=pltpu.CompilerParams(
            collective_id=0, has_side_effects=True, vmem_limit_bytes=56 * 1024 * 1024
        ),
    )(activations, out_grads, proj_in, proj_out, sample_ids, queries)
    if direct:
        return result
    return result[:, :per, :q_dev].transpose(1, 0, 2).reshape(per, half * q_dev)


def solution(mesh):
    in_specs = (
        P(("groups", "dp"), "tensor"),
        P("pipe", ("groups", "dp"), "tensor"),
        P("pipe", None, "tensor"),
        P("pipe", None, "tensor"),
        P(("groups", "dp"), None),
        P("pipe", ("dp", "tensor"), None),
    )
    out_specs = P(("groups", "dp", "tensor"), "pipe")
    return jax.shard_map(
        functools.partial(body, mesh.shape["dp"], mesh.shape["tensor"]),
        mesh=mesh, in_specs=in_specs, out_specs=out_specs, check_vma=False,
    )
```

```python
import functools

import jax
import jax.numpy as jnp
from jax import lax
from jax.experimental import pallas as pl
from jax.experimental.pallas import tpu as pltpu
from jax.sharding import PartitionSpec as P

MESH = pl.DeviceIdType.MESH
SAMP_DEV = 8
NT_DIMS = (((1,), (1,)), ((), ()))
NN_DIMS = (((1,), (0,)), ((), ()))
DAMP = 0.1
NEWTON_STEPS = 7
PIECES = 1
CHUNK = 256
AHEAD = 4


def dot_nt(a, b):
    return lax.dot_general(a, b, NT_DIMS, preferred_element_type=jnp.float32)


def project(w, x):
    return dot_nt(x, w)


def finish(part):
    return part.T


def dot_full(a, b):
    return lax.dot_general(
        a, b, NN_DIMS, precision=lax.Precision.HIGHEST, preferred_element_type=jnp.float32
    )


def each(count, step):
    if count <= 16:
        for i in range(count):
            step(i)
    else:
        lax.fori_loop(0, count, lambda i, c: (step(i), c)[1], 0)


def each_partner(n, step):
    if n <= 16:
        for s in sorted(range(1, n), key=lambda s: abs(s - n // 2)):
            step(s)
    else:
        lax.fori_loop(1, n, lambda s, c: (step(s), c)[1], 0)


def block_diag(packed, low):
    zero = jnp.zeros_like(packed)
    return jnp.concatenate([jnp.where(low, packed, zero), jnp.where(low, zero, packed)], axis=0)


def kernel(
    n_dp, n_t, dims,
    act, og, w_in, w_out, ids, qry, out,
    og_v, act_v, wi_v, wo_v, ids_v, q_v,
    rs_send, rs_recv, own, uv, fac, sg, sg_recv, inv, pre, pre32, s_send, s_recv,
    in_sem, par_sem, rs_ss, rs_rs, f_ss, f_rs, g_ss, g_rs, p_ss, p_rs, o_ss, o_rs,
):
    rank, tok, chunk, per, q_dev = dims
    n = n_dp * n_t
    half = n // 2
    part = tok // n_t
    n_chunk = part // chunk
    my_dp, my_t, my_p = lax.axis_index("dp"), lax.axis_index("tensor"), lax.axis_index("pipe")
    me = my_dp * n_t + my_t

    def at(index, pipe):
        return {"dp": lax.div(index, n_t), "tensor": lax.rem(index, n_t), "pipe": pipe}

    order = [(s, c) for s in list(range(1, n_t)) + [0] for c in range(n_chunk)]

    def chunk_copies(k):
        s, c = order[k]
        start = pl.multiple_of(lax.rem(my_t + s, n_t) * part + c * chunk, chunk)
        rows = pl.ds(start, chunk)
        deep = og_v.shape[2] // PIECES
        cuts = [pl.ds(i * deep, deep) for i in range(PIECES)]
        return [pltpu.make_async_copy(act.at[rows, :], act_v.at[k], in_sem.at[PIECES, k])] + [
            pltpu.make_async_copy(og.at[0, rows, cut], og_v.at[k, :, cut], in_sem.at[i, k])
            for i, cut in enumerate(cuts)
        ]

    load_wo = pltpu.make_async_copy(w_out.at[0], wo_v, par_sem.at[0])
    load_wi = pltpu.make_async_copy(w_in.at[0], wi_v, par_sem.at[1])
    load_ids = pltpu.make_async_copy(ids, ids_v, par_sem.at[2])
    load_q = pltpu.make_async_copy(qry.at[0], q_v, par_sem.at[3])
    load_wi.start()
    copies = [copy for k in range(len(order)) for copy in chunk_copies(k)]
    copies = copies[:1] + [load_wo] + copies[1:] + [load_ids, load_q]
    for copy in copies[:AHEAD]:
        copy.start()
    arrived = [0]

    def take():
        i = arrived[0]
        copies[i].wait()
        if i + AHEAD < len(copies):
            copies[i + AHEAD].start()
        arrived[0] = i + 1

    barrier = pltpu.get_barrier_semaphore()

    def greet(k):
        other = lax.rem(me * 2 + my_p + 1 + k, 2 * n)
        pl.semaphore_signal(
            barrier, inc=1, device_id=at(lax.div(other, 2), lax.rem(other, 2)), device_id_type=MESH
        )

    each(2 * n - 1, greet)

    def rs_copy(k):
        s, c = order[k]
        return pltpu.make_async_remote_copy(
            src_ref=rs_send.at[k], dst_ref=rs_recv.at[k],
            send_sem=rs_ss.at[k], recv_sem=rs_rs.at[k],
            device_id={"tensor": lax.rem(my_t + s, n_t)}, device_id_type=MESH,
        )

    n_send = (n_t - 1) * n_chunk
    ready = min(n_send, 2) - 1
    load_wi.wait()
    for k, (s, c) in enumerate(order):
        take()
        part_v = project(wi_v[...], act_v[k])
        if k == 0:
            take()
        part_u = 0.0
        deep = og_v.shape[2] // PIECES
        for i in range(PIECES):
            take()
            cut = slice(i * deep, (i + 1) * deep)
            part_u = part_u + project(wo_v[:, cut], og_v[k, :, cut])
        part_u, part_v = finish(part_u), finish(part_v)
        if s > 0:
            rs_send[k, :rank, :] = part_u.astype(jnp.bfloat16)
            rs_send[k, rank:, :] = part_v.astype(jnp.bfloat16)
            if k == ready:
                pl.semaphore_wait(barrier, 2 * n - 1)
                for earlier in range(k):
                    rs_copy(earlier).start()
            if k >= ready:
                rs_copy(k).start()
        else:
            own[c, :rank, :] = part_u
            own[c, rank:, :] = part_v

    for k in range(n_send):
        rs_copy(k).wait_recv()
    for c in range(n_chunk):
        total = own[c]
        for s in range(1, n_t):
            total = total + rs_recv[(s - 1) * n_chunk + c].astype(jnp.float32)
        uv[:, c * chunk:(c + 1) * chunk] = total.astype(jnp.bfloat16)

    lane = lax.broadcasted_iota(jnp.int32, (rank, 2 * rank), 1)
    row = lax.broadcasted_iota(jnp.int32, (rank, 2 * rank), 0)
    low = lane < rank
    column = lax.rem(lane, rank)
    diag = column == row
    low_half = low[: rank // 2]
    both = uv[...]
    square = dot_nt(both, both)
    packed = jnp.where(low, square[:rank], square[rank:])
    other = pltpu.roll(packed, rank, 1)
    mixed = jnp.where(low == (row < column), packed, other)
    first_diag = jnp.sum(jnp.where(diag, packed, 0.0), axis=0, keepdims=True)
    fac[0, : rank // 2, :] = jnp.where(low_half, mixed[: rank // 2], mixed[rank // 2:])
    fac[0, rank // 2:, :] = jnp.broadcast_to(first_diag, (8, 2 * rank))

    def f_copy(s):
        return pltpu.make_async_remote_copy(
            src_ref=fac.at[0], dst_ref=fac.at[s], send_sem=f_ss.at[s], recv_sem=f_rs.at[s],
            device_id=at(lax.rem(me + s, n), my_p), device_id_type=MESH,
        )

    each_partner(n, lambda s: f_copy(s).start())

    take()
    own_ids = ids_v[:, pl.ds(pl.multiple_of(my_t * part, 128), part)]
    u_rows, v_rows = uv[:rank, :], uv[rank:, :]

    def g_copy(s):
        return pltpu.make_async_remote_copy(
            src_ref=sg.at[s], dst_ref=sg_recv.at[s - 1], send_sem=g_ss.at[s - 1], recv_sem=g_rs.at[s - 1],
            device_id={"tensor": lax.rem(my_t + s, n_t)}, device_id_type=MESH,
        )

    wide = max(2, per)
    for s in list(range(1, n_t)) + [0]:
        first = lax.rem(my_t + s, n_t) * per
        masked = jnp.concatenate(
            [jnp.where(own_ids == first + i, v_rows.astype(jnp.float32), 0.0) for i in range(wide)], axis=0
        ).astype(jnp.bfloat16)
        sg[s] = dot_nt(u_rows, masked)
        if s > 0:
            g_copy(s).start()

    each(n - 1, lambda k: f_copy(k + 1).wait_recv())
    if n <= 16:
        factor = fac[0]
        for k in range(1, n):
            factor = factor + fac[k]
    else:
        factor = lax.fori_loop(1, n, lambda k, f: f + fac[k], fac[0])
    folded = factor[: rank // 2]
    turned = pltpu.roll(folded, rank, 1)
    mixed = jnp.concatenate(
        [jnp.where(low_half, folded, turned), jnp.where(low_half, turned, folded)], axis=0
    )
    mirrored = jnp.concatenate([mixed, mixed], axis=0).T[:rank]
    first_diag = factor[rank // 2: rank // 2 + 1]
    factor = jnp.where(low == (row < column), mixed, mirrored)
    factor = jnp.where(diag, jnp.where(low, first_diag, mixed), factor)
    factor = factor * (1.0 / (tok * n_dp))
    on_diag = jnp.sum(jnp.where(diag, factor, 0.0), axis=0, keepdims=True)
    lane1 = lax.broadcasted_iota(jnp.int32, (1, 2 * rank), 1)
    trace_a = jnp.sum(jnp.where(lane1 < rank, on_diag, 0.0), axis=1, keepdims=True)
    trace_b = jnp.sum(jnp.where(lane1 < rank, 0.0, on_diag), axis=1, keepdims=True)
    trace = jnp.where(lane1 < rank, trace_a, trace_b)
    eye = jnp.where(diag, 1.0, 0.0)
    damped = factor + (DAMP / rank) * trace * eye
    least = (DAMP / rank) / (1.0 + DAMP / rank)
    alpha = 2.0 / (1.0 + least)
    bound = least * alpha
    scale = alpha / ((1.0 + DAMP / rank) * trace)
    state = jnp.concatenate([damped * scale, eye * scale], axis=0)
    for _ in range(NEWTON_STEPS):
        beta = 2.0 / (1.0 + bound * (2.0 - bound))
        bound = beta * bound * (2.0 - bound)
        state = beta * dot_full(state, block_diag(2.0 * eye - state[:rank], low))
    x = state[rank:]
    t = dot_full(damped, block_diag(x, low))
    x = dot_full(x, block_diag(2.0 * eye - t, low))
    inv[...] = x

    for s in range(1, n_t):
        g_copy(s).wait_recv()
    grads = sg[0]
    for s in range(1, n_t):
        grads = grads + sg_recv[s - 1]
    even = inv[pl.ds(0, rank // 2, stride=2), :]
    odd = inv[pl.ds(1, rank // 2, stride=2), :]
    left = jnp.where(low_half, even, pltpu.roll(odd, rank, 1))
    x_in = jnp.where(low, pltpu.roll(x, rank, 1), x)
    right = block_diag(x_in, low)
    blocks = []
    for m in range(wide // 2):
        pair = grads[:, m * 2 * rank:(m + 1) * 2 * rank]
        swapped = pltpu.roll(pair, rank, 1)
        blocks.append(block_diag(jnp.where(low, pair, swapped), low))
        blocks.append(block_diag(jnp.where(low, swapped, pair), low))
    blocks = blocks[:per]
    mid = dot_full(left, jnp.concatenate(blocks, axis=1))
    mid = jnp.concatenate([mid[:, i * 2 * rank:(i + 1) * 2 * rank] for i in range(per)], axis=0)
    pre[me] = dot_full(mid, right).astype(jnp.bfloat16)

    def p_copy(s):
        return pltpu.make_async_remote_copy(
            src_ref=pre.at[me], dst_ref=pre.at[me], send_sem=p_ss.at[s], recv_sem=p_rs.at[s],
            device_id=at(lax.rem(me + s, n), my_p), device_id_type=MESH,
        )

    each_partner(n, lambda s: p_copy(s).start())
    each(n - 1, lambda k: p_copy(k + 1).wait_recv())

    fine = rank // 2
    total_samples = n * per
    pre32[...] = pre[...].astype(jnp.float32).reshape(total_samples * fine, 2 * rank)
    flat = jnp.concatenate(
        [pre32[pl.ds(a, total_samples, stride=fine), :].astype(jnp.bfloat16) for a in range(fine)], axis=1
    )
    take()
    scores = dot_nt(flat, q_v[...])
    for j in range(n):
        s_send[j, :per, :q_dev] = scores[j * per:(j + 1) * per]

    my_half = lax.div(me, half)
    slot = my_p * half + lax.rem(me, half)

    def o_copy(s):
        j = lax.rem(me + s, n)
        return pltpu.make_async_remote_copy(
            src_ref=s_send.at[j], dst_ref=s_recv.at[slot], send_sem=o_ss.at[s], recv_sem=o_rs.at[slot],
            device_id=at(j, my_half), device_id_type=MESH,
        )

    each_partner(n, lambda s: o_copy(s).start())

    @pl.when(my_half == my_p)
    def _():
        s_recv[slot] = s_send[me]

    @pl.when(my_half != my_p)
    def _():
        o_copy(0).start()

    def o_wait(k):
        source = my_p * half + lax.rem(k, half)

        @pl.when(jnp.logical_or(source != me, lax.div(k, half) != my_p))
        def _():
            pltpu.make_async_remote_copy(
                src_ref=s_send.at[0], dst_ref=s_recv.at[k], send_sem=o_ss.at[0], recv_sem=o_rs.at[k],
                device_id=at(lax.rem(me + 1, n), my_p), device_id_type=MESH,
            ).wait_recv()

    each(n, o_wait)
    if q_dev % 128 == 0:
        for k in range(half):
            out[:, k * q_dev:(k + 1) * q_dev] = (s_recv[k] + s_recv[half + k])[:per, :q_dev]
    else:
        out[...] = s_recv[:half] + s_recv[half:]

    for k in range(n_send):
        rs_copy(k).wait_send()
    each(n - 1, lambda k: f_copy(k + 1).wait_send())
    for s in range(1, n_t):
        g_copy(s).wait_send()
    each(n - 1, lambda k: p_copy(k + 1).wait_send())
    each(n - 1, lambda k: o_copy(k + 1).wait_send())

    @pl.when(my_half != my_p)
    def _():
        o_copy(0).wait_send()


def body(n_dp, n_t, activations, out_grads, proj_in, proj_out, sample_ids, queries):
    rank = proj_in.shape[1]
    tok, width = activations.shape
    hidden = out_grads.shape[2]
    q_dev, feat = queries.shape[1:]
    n = n_dp * n_t
    half = n // 2
    per = SAMP_DEV // n_t
    part = tok // n_t
    chunk = min(part, CHUNK)
    n_chunk = part // chunk
    n_all, n_send = n_t * n_chunk, (n_t - 1) * n_chunk
    wide = max(2, per) * rank
    lanes = max(q_dev, 128)
    direct = q_dev % 128 == 0
    out_shape = (per, half * q_dev) if direct else (half, 8, lanes)
    bf16, f32 = jnp.bfloat16, jnp.float32
    dma = pltpu.SemaphoreType.DMA
    result = pl.pallas_call(
        functools.partial(kernel, n_dp, n_t, (rank, tok, chunk, per, q_dev)),
        out_shape=jax.ShapeDtypeStruct(out_shape, f32),
        in_specs=[pl.BlockSpec(memory_space=pl.ANY)] * 6,
        out_specs=pl.BlockSpec(memory_space=pltpu.VMEM),
        scratch_shapes=[
            pltpu.VMEM((n_all, chunk, hidden), bf16),
            pltpu.VMEM((n_all, chunk, width), bf16),
            pltpu.VMEM((rank, width), bf16),
            pltpu.VMEM((rank, hidden), bf16),
            pltpu.VMEM(sample_ids.shape, jnp.int32),
            pltpu.VMEM((q_dev, feat), bf16),
            pltpu.VMEM((n_send, 2 * rank, chunk), bf16),
            pltpu.VMEM((n_send, 2 * rank, chunk), bf16),
            pltpu.VMEM((n_chunk, 2 * rank, chunk), f32),
            pltpu.VMEM((2 * rank, part), bf16),
            pltpu.VMEM((n, rank // 2 + 8, 2 * rank), f32),
            pltpu.VMEM((n_t, rank, wide), f32),
            pltpu.VMEM((n_t - 1, rank, wide), f32),
            pltpu.VMEM((rank, 2 * rank), f32),
            pltpu.VMEM((n, per * rank // 2, 2 * rank), bf16),
            pltpu.VMEM((n * per * rank // 2, 2 * rank), f32),
            pltpu.VMEM((n, 8, lanes), f32),
            pltpu.VMEM((n, 8, lanes), f32),
            dma((PIECES + 1, n_all)), dma((4,)),
            dma((n_send,)), dma((n_send,)),
            dma((n,)), dma((n,)),
            dma((n_t - 1,)), dma((n_t - 1,)),
            dma((n,)), dma((n,)),
            dma((n,)), dma((n,)),
        ],
        compiler_params=pltpu.CompilerParams(
            collective_id=0, has_side_effects=True, vmem_limit_bytes=56 * 1024 * 1024
        ),
    )(activations, out_grads, proj_in, proj_out, sample_ids, queries)
    if direct:
        return result
    return result[:, :per, :q_dev].transpose(1, 0, 2).reshape(per, half * q_dev)


def solution(mesh):
    in_specs = (
        P(("groups", "dp"), "tensor"),
        P("pipe", ("groups", "dp"), "tensor"),
        P("pipe", None, "tensor"),
        P("pipe", None, "tensor"),
        P(("groups", "dp"), None),
        P("pipe", ("dp", "tensor"), None),
    )
    out_specs = P(("groups", "dp", "tensor"), "pipe")
    return jax.shard_map(
        functools.partial(body, mesh.shape["dp"], mesh.shape["tensor"]),
        mesh=mesh, in_specs=in_specs, out_specs=out_specs, check_vma=False,
    )
```
